32 devices in a mesh: groups: 2 (over x), gx: 16 (over z, y, core).
Axes of the slice: x: 2, y: 2, z: 4, core: 2. Of those that a mesh axis runs over, the one named last changes fastest.
Arguments:
- spectrum: float32 [30, 24, 16, 2048], P(None, None, 'groups', 'gx'), parts along dimension 2, may hold values from 0.01 to 1
- sea_mask: int32 [16, 2048], P('groups', 'gx'), parts along dimension 0, may hold values 0 or 1
- courant: float32 [30], replicated, may hold values from 0.35 to 0.7
- phase_speed: float32 [30], replicated, may hold values from 1.5 to 15
- growth_rate: float32 [30], replicated, may hold values from 0.02 to 0.2
- dissipation: float32 [30], replicated, may hold values from 0.002 to 0.02
- atmos_fields: float32 [16, 4, 8, 1024], P('gx', None, 'groups'), parts along dimension 2, may hold values from -24 to 24, as said below
- intersection_tile: int32 [4, 16, 2048], P(None, 'groups', 'gx'), parts along dimension 1, may hold values from 0 to 15, as said below
- intersection_cell: int32 [4, 16, 2048], P(None, 'groups', 'gx'), parts along dimension 1, may hold values from 0 to 1023
- intersection_weight: float32 [4, 16, 2048], P(None, 'groups', 'gx'), parts along dimension 1, may hold values from 0.1 to 0.4
Outputs:
- wave_spectrum: float32 [30, 24, 16, 2048], P(None, None, 'groups', 'gx'), parts along dimension 2
- atmos_roughness: float32 [16, 8, 1024], P('gx', 'groups'), parts along dimension 1
The draws below stay inside these ranges and needn't reach their ends.
There are 2 independent parts, one for each index of `groups`. The reference program is written for one: setup_inputs(seed, part) draws one part's arguments, and reference() takes and returns one part's arrays. A program takes and returns all parts, laid end to end along the dimension named above; an argument that names none is the same for every part. Nothing has to cross between parts.
Inputs may be any that keep to these rules, and one draw needn't show every extreme that they name: `intersection_tile`: the tile of every intersection of a wave cell in column x is b * 4 + x // 512 for some b in 0 .. 3. `atmos_fields`: fields 0 and 1 are winds, field 2 lies in 1.1 to 1.3, field 3 in -1 to 1.
All inputs are finite; a program needn't handle non-finite values. No bound on the sum of `sea_mask` on one device may be relied on, other than what follows from the above.
Results may differ from the reference program's by a relative error of at most 0.00002.
Values sent between devices are 32-bit elements; how exact they have to be, the bound alone decides.
A program may use at most 128 MiB of HBM per device.

```python
import math
import jax
import jax.numpy as jnp
from jax import lax

FREQS = 30
DIRS = 24
LAT = 8
BX = 128
ATY = 4
SUBSTEPS = 2
NX = 2048
TILES = 16


def intersection_lists(key):
    band_rows = 2 * LAT // ATY
    lon_bands = TILES // ATY
    row_shift = jax.random.randint(key, (LAT, NX), 0, 2, dtype=jnp.int32)
    row_index = jnp.arange(LAT, dtype=jnp.int32)[:, None]
    col_index = jnp.arange(NX, dtype=jnp.int32)[None, :]
    start_row = jnp.clip(2 * row_index - 1 + row_shift, 0, 2 * LAT - 2)
    group_index = col_index // BX // ATY
    tiles = []
    cells = []
    for intersection in range(4):
        atmos_row = start_row + intersection // 2
        tiles.append(atmos_row // band_rows * lon_bands + group_index)
        cells.append(atmos_row % band_rows * (2 * BX) + 2 * (col_index % BX) + intersection % 2)
    return (jnp.stack(tiles).astype(jnp.int32), jnp.stack(cells).astype(jnp.int32))


def draw_intersection_tile(key, part):
    tiles, cells = intersection_lists(key)
    return tiles


def draw_intersection_cell(key, part):
    tiles, cells = intersection_lists(key)
    return cells


def draw_atmos_fields(key, part):
    key = jax.random.fold_in(key, 7)
    shape = (TILES, 2 * LAT // ATY, 2 * BX * ATY)
    first, second, third, fourth = jax.random.split(key, 4)
    east_wind = 8.0 * jnp.clip(jax.random.normal(first, shape, jnp.float32), -3.0, 3.0)
    north_wind = 8.0 * jnp.clip(jax.random.normal(second, shape, jnp.float32), -3.0, 3.0)
    air_density = jax.random.uniform(third, shape, jnp.float32, 1.1, 1.3)
    stability = jax.random.uniform(fourth, shape, jnp.float32, -1.0, 1.0)
    return jnp.stack([east_wind, north_wind, air_density, stability], axis=1)


def with_ends(values, stream_key, low, high):
    longest = values.shape.index(max(values.shape))
    spots = []
    for shift in (0, 1):
        where = [jax.random.randint(jax.random.fold_in(stream_key, axis), (), 0, length) for axis, length in enumerate(values.shape)]
        where[longest] = (where[longest] + shift) % values.shape[longest]
        spots.append(tuple(where))
    return values.at[spots[0]].set(low).at[spots[1]].set(high)


def levels(key, extent, pieces, low, largest):
    level = 1.0
    for position, blocks in pieces:
        steps = jax.random.uniform(jax.random.fold_in(jax.random.fold_in(key, 6), position), (blocks,), jnp.float32, low / len(pieces), largest / len(pieces))
        level = level * jnp.repeat(jnp.exp(steps), extent[position] // blocks).reshape((-1,) + (1,) * (len(extent) - 1 - position))
    return level


def setup_inputs(seed: int = 0, part: int = 0) -> dict:
    splits = jax.random.split(jax.random.key(seed), 11)
    part_keys = jax.random.split(jax.random.fold_in(splits[10], part), 11)
    return {
        "spectrum": jnp.clip(jnp.exp(math.log(1.0) - 4.6051702 * jax.random.uniform(part_keys[0], (FREQS, DIRS, LAT, NX), jnp.float32) ** levels(part_keys[0], (FREQS, DIRS, LAT, NX), ((3, 16),), -0.2, 0.2)), 0.01, 1.0),
        "sea_mask": with_ends((jax.random.randint(part_keys[1], (LAT, NX), 0, 4) < 3).astype(jnp.int32), jax.random.fold_in(part_keys[1], 1), 0, 1),
        "courant": jnp.clip(jax.random.uniform(splits[2], (FREQS,), jnp.float32, 0.35, 0.7), 0.35, 0.7),
        "phase_speed": jnp.clip(jnp.exp(jax.random.uniform(splits[3], (FREQS,), jnp.float32, math.log(1.5), math.log(15.0))), 1.5, 15.0),
        "growth_rate": jnp.clip(jnp.exp(jax.random.uniform(splits[4], (FREQS,), jnp.float32, math.log(0.02), math.log(0.2))), 0.02, 0.2),
        "dissipation": jnp.clip(jnp.exp(jax.random.uniform(splits[5], (FREQS,), jnp.float32, math.log(0.002), math.log(0.02))), 0.002, 0.02),
        "atmos_fields": draw_atmos_fields(jax.random.fold_in(jax.random.fold_in(splits[10], part), 71), part),
        "intersection_tile": draw_intersection_tile(jax.random.fold_in(jax.random.fold_in(splits[10], part), 71), part),
        "intersection_cell": draw_intersection_cell(jax.random.fold_in(jax.random.fold_in(splits[10], part), 71), part),
        "intersection_weight": jnp.clip(0.1 + 0.3 * jax.random.uniform(part_keys[9], (4, LAT, NX), jnp.float32) ** levels(part_keys[9], (4, LAT, NX), ((2, 16),), -0.2, 0.2), 0.1, 0.4),
    }


def advance(padded, sea_frac, step_x, step_y):
    center = padded[..., 1:-1]
    west_cell = padded[..., :-2]
    east_cell = padded[..., 2:]
    zero_row = jnp.zeros_like(center[..., :1, :])
    south_cell = jnp.concatenate([zero_row, center[..., :-1, :]], axis=-2)
    north_cell = jnp.concatenate([center[..., 1:, :], zero_row], axis=-2)
    result = center - jnp.maximum(step_x, 0.0) * (center - west_cell)
    result = result - jnp.maximum(-step_x, 0.0) * (center - east_cell)
    result = result - jnp.maximum(step_y, 0.0) * (center - south_cell)
    result = result - jnp.maximum(-step_y, 0.0) * (center - north_cell)
    return sea_frac * result


def reference(spectrum, sea_mask, courant, phase_speed, growth_rate, dissipation, atmos_fields, intersection_tile, intersection_cell, intersection_weight):
    dir_count = spectrum.shape[1]
    total_cols = spectrum.shape[3]
    angles = jnp.arange(dir_count, dtype=jnp.float32) * (2.0 * math.pi / dir_count)
    cosine = jnp.cos(angles)
    sine_dir = jnp.sin(angles)
    sea_frac = sea_mask.astype(jnp.float32)

    def propagate(inputs):
        freq_plane, speed_value = inputs
        step_x = (speed_value * cosine)[:, None, None]
        step_y = (speed_value * sine_dir)[:, None, None]
        field = freq_plane * sea_frac
        for substep in range(SUBSTEPS):
            padded = jnp.concatenate([field[..., -1:], field, field[..., :1]], axis=-1)
            field = advance(padded, sea_frac, step_x, step_y)
        return field

    field = lax.map(propagate, (spectrum, courant))
    col_index = jnp.arange(total_cols, dtype=jnp.int32)
    col_base = ((col_index // BX) % ATY) * (2 * BX)
    atmos_row = (intersection_cell // (2 * BX)).astype(jnp.int32)
    atmos_col = (col_base[None, None, :] + intersection_cell % (2 * BX)).astype(jnp.int32)
    forcing = [jnp.sum(intersection_weight * atmos_fields[intersection_tile, which, atmos_row, atmos_col], axis=0) for which in range(4)]
    east_wind, north_wind, air_density, stability = forcing
    energy = jnp.sum(field, axis=(0, 1))
    along = cosine[:, None, None] * east_wind + sine_dir[:, None, None] * north_wind
    boost = jnp.exp(0.3 * stability)

    def sources(inputs):
        freq_plane, phase_value, rate_value, decay_value = inputs
        growth = rate_value * air_density * jnp.maximum(along / phase_value - 1.0, 0.0) * boost
        updated = freq_plane * (1.0 + growth) / (1.0 + decay_value * energy)
        return updated, jnp.sum(growth * updated, axis=0)

    updated, stress_parts = lax.map(sources, (field, phase_speed, growth_rate, dissipation))
    stress = jnp.sum(stress_parts, axis=0)
    surface = 0.01 * (east_wind * east_wind + north_wind * north_wind + stress)
    contribution = intersection_weight * sea_frac * surface
    roughness = jnp.zeros((TILES, atmos_fields.shape[2], atmos_fields.shape[3]), jnp.float32)
    roughness = roughness.at[intersection_tile, atmos_row, atmos_col].add(contribution)
    return updated, roughness
```

```python
import functools
import math

import jax
import jax.numpy as jnp
import numpy as np
from jax import lax
from jax.experimental import pallas as pl
from jax.experimental.pallas import tpu as pltpu
from jax.sharding import PartitionSpec as P

ATY = 4
FCHUNK = 5
MESH = pl.DeviceIdType.MESH


def directions(count):
    angles = np.arange(count, dtype=np.float32) * np.float32(2.0 * math.pi / count)
    cosine, sine = np.cos(angles), np.sin(angles)
    forward = [d for d in range(count) if cosine[d] >= 0]
    backward = [d for d in range(count) if cosine[d] < 0]
    return cosine, sine, forward, backward


def pack_constants(dirs, slots):
    cosine, sine, forward, backward = directions(dirs)
    table = np.zeros((2, 3, 8, 128), np.float32)
    for side, members in enumerate((forward, backward)):
        for fi in range(FCHUNK):
            for k, d in enumerate(members):
                lane = fi * slots + 2 * k
                table[side, 0, :, lane : lane + 2] = abs(cosine[d])
                table[side, 1, :, lane : lane + 2] = max(sine[d], 0.0)
                table[side, 2, :, lane : lane + 2] = max(-sine[d], 0.0)
    return table


def lane_row(shape):
    lane = lax.broadcasted_iota(jnp.int32, shape, 1)
    row = lax.broadcasted_iota(jnp.int32, shape, 0)
    return lane, row


def exchange_kernel(
    ranks,
    spec_hbm,
    sea_ref,
    courant_ref,
    const_ref,
    atmos_ref,
    table_ref,
    west_ref,
    east_ref,
    spec,
    pack,
    in_sem,
    piece_send,
    piece_recv,
    halo_send,
    halo_recv,
):
    freqs, dirs = spec.shape[0], spec.shape[1]
    chunks = freqs // FCHUNK
    _, _, forward, backward = directions(dirs)
    slots = 2 * len(forward)
    me = lax.axis_index("gx")
    bands = ranks // ATY
    east, west = lax.rem(me + 1, ranks), lax.rem(me + ranks - 1, ranks)
    group, band = me // ATY, me // bands
    first_target = lax.rem(me, bands) * ATY
    own = lax.rem(me, bands) == group

    def load(g):
        span = pl.ds(g * FCHUNK, FCHUNK)
        return pltpu.make_async_copy(spec_hbm.at[span], spec.at[span], in_sem.at[g])

    for g in range(chunks):
        load(g).start()

    barrier = pltpu.get_barrier_semaphore()
    for device in (east, west):
        pl.semaphore_signal(barrier, inc=1, device_id={"gx": device}, device_id_type=MESH)
    for b in range(ATY):
        source = b * bands + group

        @pl.when(source != me)
        def _():
            pl.semaphore_signal(barrier, inc=1, device_id={"gx": source}, device_id_type=MESH)

    pl.semaphore_wait(barrier, 2 + ATY - own.astype(jnp.int32))

    span = atmos_ref.shape[3] // ATY

    def piece(j):
        return atmos_ref.at[0, :, :, pl.ds(j * span, span)]

    def piece_copy(j):
        return pltpu.make_async_remote_copy(
            src_ref=piece(j),
            dst_ref=table_ref.at[band],
            send_sem=piece_send.at[j],
            recv_sem=piece_recv.at[band],
            device_id={"gx": first_target + j},
            device_id_type=MESH,
        )

    for j in range(ATY):

        @pl.when(first_target + j != me)
        def _():
            piece_copy(j).start()

        @pl.when(first_target + j == me)
        def _():
            pltpu.make_async_copy(piece(j), table_ref.at[band], piece_recv.at[band]).start()

    lane, row = lane_row((8, 128))
    half = lane // 2
    odd = lane % 2 == 1
    sea = sea_ref[...].astype(jnp.float32)

    def tiled(shift):
        out = jnp.where(lane < 2, pltpu.roll(sea, shift, 1), 0.0)
        for step in (2, 4, 8, 16, 32, 64):
            out = out + pltpu.roll(out, step, 1)
        return out

    sea_pair = (tiled(2), tiled(0))
    freq_of_lane = lane // slots

    def chunk(g, carry):
        load(g).wait()
        acc = [jnp.zeros((8, 128), jnp.float32) for _ in range(2)]
        speed = jnp.zeros((8, 128), jnp.float32)
        for fi in range(FCHUNK):
            f = g * FCHUNK + fi
            speed = jnp.where(freq_of_lane == fi, courant_ref[f], speed)
            for side, members in enumerate((forward, backward)):
                for k, d in enumerate(members):
                    at = fi * slots + 2 * k
                    shift = (at + (2 if side == 0 else 0)) % 128
                    value = spec[f, d]
                    if shift:
                        value = pltpu.roll(value, shift, 1)
                    acc[side] = jnp.where(half == at // 2, value, acc[side])
        for side in range(2):
            field = acc[side] * sea_pair[side]
            upwind = pltpu.roll(field, 1 if side == 0 else 127, 1)
            south = jnp.where(row == 0, 0.0, pltpu.roll(field, 1, 0))
            north = jnp.where(row == 7, 0.0, pltpu.roll(field, 7, 0))
            later = field - speed * const_ref[side, 0] * (field - upwind)
            later = later - speed * const_ref[side, 1] * (field - south)
            later = later - speed * const_ref[side, 2] * (field - north)
            later = later * sea_pair[side]
            if side == 0:
                both = jnp.where(odd, later, pltpu.roll(field, 127, 1))
            else:
                both = jnp.where(odd, pltpu.roll(field, 1, 1), later)
            pack[side, g] = both
        return carry

    lax.fori_loop(0, chunks, chunk, 0)

    to_east = pltpu.make_async_remote_copy(
        src_ref=pack.at[0],
        dst_ref=west_ref,
        send_sem=halo_send.at[0],
        recv_sem=halo_recv.at[0],
        device_id={"gx": east},
        device_id_type=MESH,
    )
    to_west = pltpu.make_async_remote_copy(
        src_ref=pack.at[1],
        dst_ref=east_ref,
        send_sem=halo_send.at[1],
        recv_sem=halo_recv.at[1],
        device_id={"gx": west},
        device_id_type=MESH,
    )
    to_east.start()
    to_west.start()

    for j in range(ATY):

        @pl.when(first_target + j != me)
        def _():
            piece_copy(j).wait_send()

    for b in range(ATY):
        pltpu.make_async_copy(table_ref.at[b], table_ref.at[b], piece_recv.at[b]).wait()
    to_east.wait()
    to_west.wait()


def wave_kernel(
    bands,
    spec_hbm,
    sea_ref,
    courant_ref,
    phase_ref,
    rate_ref,
    decay_ref,
    tile_ref,
    cell_ref,
    weight_ref,
    table_ref,
    west_ref,
    east_ref,
    out_hbm,
    stress_ref,
    spec,
    out,
    along_ref,
    lane_hot,
    row_hot,
    in_sem,
    out_sem,
):
    freqs, dirs = spec.shape[0], spec.shape[1]
    chunks = freqs // FCHUNK
    cosine, sine, forward, backward = directions(dirs)
    slots = 2 * len(forward)

    def load(g):
        span = pl.ds(g * FCHUNK, FCHUNK)
        return pltpu.make_async_copy(spec_hbm.at[span], spec.at[span], in_sem.at[g])

    def store(g):
        span = pl.ds(g * FCHUNK, FCHUNK)
        return pltpu.make_async_copy(out.at[span], out_hbm.at[span], out_sem.at[g])

    for g in range(chunks):
        load(g).start()

    lane, row = lane_row((8, 128))
    sea = sea_ref[...].astype(jnp.float32)

    tile = [tile_ref[l] for l in range(4)]
    cell = [cell_ref[l] for l in range(4)]
    weight = [weight_ref[l] for l in range(4)]
    low = [c & 127 for c in cell]
    high = []
    for l in range(4):
        band = jnp.zeros((8, 128), jnp.int32)
        for b in range(1, ATY):
            band = band + (tile[l] >= b * bands).astype(jnp.int32)
        high.append(band * 8 + (cell[l] >> 7))

    forcing = [[jnp.zeros((8, 128), jnp.float32) for _ in range(4)] for _ in range(4)]
    for h in range(32):
        b, r, c = h // 8, h % 8 // 2, h % 2
        hit = [high[l] == h for l in range(4)]
        for k in range(4):
            line = jnp.broadcast_to(table_ref[b, k, pl.ds(r, 1), pl.ds(c * 128, 128)], (8, 128))
            for l in range(4):
                found = jnp.take_along_axis(line, low[l], axis=1)
                forcing[k][l] = jnp.where(hit[l], found, forcing[k][l])
    east_wind, north_wind, air, stability = [
        (weight[0] * v[0] + weight[1] * v[1]) + (weight[2] * v[2] + weight[3] * v[3])
        for v in forcing
    ]
    for d in range(dirs):
        along_ref[d] = float(cosine[d]) * east_wind + float(sine[d]) * north_wind

    lows = lax.broadcasted_iota(jnp.int32, (128, 128), 0)
    for l in range(4):
        for y in range(8):
            at = pl.ds((l * 8 + y) * 128, 128)
            same = lows == jnp.broadcast_to(low[l][y : y + 1], (128, 128))
            lane_hot[:, at] = jnp.where(same, 1.0, 0.0).astype(jnp.bfloat16)

    first, last = lane == 0, lane == 127
    bottom, top = row == 0, row == 7

    def propagate(g, energy):
        load(g).wait()
        sums = [energy] + [jnp.zeros((8, 128), jnp.float32) for _ in range(3)]
        halos = (west_ref[g], east_ref[g])
        turn = 0
        for fi in range(FCHUNK):
            f = g * FCHUNK + fi
            speed = courant_ref[f]
            for side, members in enumerate((forward, backward)):
                for k, d in enumerate(members):
                    at = fi * slots + 2 * k
                    halo = pltpu.roll(halos[side], (127 - at) % 128, 1)
                    step_x = speed * float(abs(cosine[d]))
                    step_y = speed * float(abs(sine[d]))
                    keep = 1.0 - step_x - step_y
                    shift = 1 if side == 0 else 127
                    field = spec[f, d] * sea
                    for substep in range(2):
                        if substep == 0:
                            upwind = jnp.where(last if side == 0 else first, halo, field)
                            upwind = pltpu.roll(upwind, shift, 1)
                        else:
                            upwind = pltpu.roll(field, shift, 1)
                            upwind = jnp.where(first if side == 0 else last, halo, upwind)
                        result = keep * field + step_x * upwind
                        if sine[d] != 0:
                            up = sine[d] > 0
                            beside = pltpu.roll(field, 1 if up else 7, 0)
                            beside = jnp.where(bottom if up else top, 0.0, beside)
                            result = result + step_y * beside
                        field = sea * result
                    out[f, d] = field
                    sums[turn % 4] = sums[turn % 4] + field
                    turn += 1
        return (sums[0] + sums[1]) + (sums[2] + sums[3])

    energy = lax.fori_loop(0, chunks, propagate, jnp.zeros((8, 128), jnp.float32))

    base = air * jnp.exp(0.3 * stability)

    def sources(g, stress):
        sums = [stress] + [jnp.zeros((8, 128), jnp.float32) for _ in range(3)]
        for fi in range(FCHUNK):
            f = g * FCHUNK + fi
            offset = rate_ref[f] * base
            slope = offset / phase_ref[f]
            scale = 1.0 / (1.0 + decay_ref[f] * energy)
            for d in range(dirs):
                growth = jnp.maximum(along_ref[d] * slope - offset, 0.0)
                scaled = out[f, d] * scale
                updated = scaled + scaled * growth
                out[f, d] = updated
                sums[d % 4] = sums[d % 4] + growth * updated
        store(g).start()
        return (sums[0] + sums[1]) + (sums[2] + sums[3])

    stress = lax.fori_loop(0, chunks, sources, jnp.zeros((8, 128), jnp.float32))

    surface = sea * (0.01 * (east_wind * east_wind + north_wind * north_wind + stress))
    highs = lax.broadcasted_iota(jnp.int32, (32, 128), 0)
    for l in range(4):
        rest = weight[l] * surface
        parts = []
        for _ in range(3):
            part = rest.astype(jnp.bfloat16).astype(jnp.float32)
            parts.append(part)
            rest = rest - part
        for y in range(8):
            at = pl.ds((l * 8 + y) * 128, 128)
            same = highs == jnp.broadcast_to(high[l][y : y + 1], (32, 128))
            for p, part in enumerate(parts):
                line = jnp.broadcast_to(part[y : y + 1], (32, 128))
                row_hot[pl.ds(p * 32, 32), at] = jnp.where(same, line, 0.0).astype(jnp.bfloat16)
    spread = lax.dot_general(
        row_hot[...],
        lane_hot[...],
        (((1,), (1,)), ((), ())),
        preferred_element_type=jnp.float32,
    )
    stress_ref[...] = spread[0:32] + (spread[32:64] + spread[64:96])

    for g in range(chunks):
        store(g).wait()


def return_kernel(ranks, stress_ref, out_ref, landed, send_sem, recv_sem):
    me = lax.axis_index("gx")
    bands = ranks // ATY
    group = me // ATY
    slot = lax.rem(me, ATY)
    first_source = lax.rem(me, bands) * ATY
    own = lax.rem(me, bands) == group
    barrier = pltpu.get_barrier_semaphore()
    for j in range(ATY):

        @pl.when(first_source + j != me)
        def _():
            pl.semaphore_signal(
                barrier, inc=1, device_id={"gx": first_source + j}, device_id_type=MESH
            )

    pl.semaphore_wait(barrier, ATY - own.astype(jnp.int32))

    def piece(b):
        return stress_ref.at[pl.ds(b * 8, 8)]

    def piece_copy(b):
        return pltpu.make_async_remote_copy(
            src_ref=piece(b),
            dst_ref=landed.at[slot],
            send_sem=send_sem.at[b],
            recv_sem=recv_sem.at[slot],
            device_id={"gx": b * bands + group},
            device_id_type=MESH,
        )

    for b in range(ATY):

        @pl.when(b * bands + group != me)
        def _():
            piece_copy(b).start()

        @pl.when(b * bands + group == me)
        def _():
            pltpu.make_async_copy(piece(b), landed.at[slot], recv_sem.at[slot]).start()

    for j in range(ATY):
        pltpu.make_async_copy(landed.at[j], landed.at[j], recv_sem.at[j]).wait()
        for r in range(4):
            for c in range(2):
                out_ref[0, pl.ds(r, 1), pl.ds(j * 256 + c * 128, 128)] = landed[
                    j, pl.ds(2 * r + c, 1), :
                ]
    for b in range(ATY):

        @pl.when(b * bands + group != me)
        def _():
            piece_copy(b).wait_send()


def on_device(
    ranks,
    spectrum,
    sea_mask,
    courant,
    phase_speed,
    growth_rate,
    dissipation,
    atmos_fields,
    intersection_tile,
    intersection_cell,
    intersection_weight,
):
    freqs, dirs, lat, width = spectrum.shape
    chunks = freqs // FCHUNK
    bands = ranks // ATY
    f32 = jnp.float32
    _, _, forward, _ = directions(dirs)
    consts = jnp.asarray(pack_constants(dirs, 2 * len(forward)))
    anywhere = pl.BlockSpec(memory_space=pl.ANY)
    vmem = pl.BlockSpec(memory_space=pltpu.VMEM)
    smem = pl.BlockSpec(memory_space=pltpu.SMEM)
    dma = pltpu.SemaphoreType.DMA
    span = atmos_fields.shape[3] // ATY
    halo = jax.ShapeDtypeStruct((chunks, lat, width), f32)
    table, west, east = pl.pallas_call(
        functools.partial(exchange_kernel, ranks),
        out_shape=(
            jax.ShapeDtypeStruct((ATY,) + atmos_fields.shape[1:3] + (span,), f32),
            halo,
            halo,
        ),
        in_specs=[anywhere, vmem, smem, vmem, anywhere],
        out_specs=(anywhere, anywhere, anywhere),
        scratch_shapes=[
            pltpu.VMEM(spectrum.shape, f32),
            pltpu.VMEM((2, chunks, lat, width), f32),
            dma((chunks,)),
            dma((ATY,)),
            dma((ATY,)),
            dma((2,)),
            dma((2,)),
        ],
        compiler_params=pltpu.CompilerParams(
            collective_id=0, has_side_effects=True, vmem_limit_bytes=16 * 2**20
        ),
        name="exchange",
    )(spectrum, sea_mask, courant, consts, atmos_fields)

    updated, stress = pl.pallas_call(
        functools.partial(wave_kernel, bands),
        out_shape=(
            jax.ShapeDtypeStruct(spectrum.shape, f32),
            jax.ShapeDtypeStruct((32, 128), f32),
        ),
        in_specs=[anywhere, vmem, smem, smem, smem, smem] + [vmem] * 6,
        out_specs=(anywhere, vmem),
        scratch_shapes=[
            pltpu.VMEM(spectrum.shape, f32),
            pltpu.VMEM(spectrum.shape, f32),
            pltpu.VMEM((dirs, lat, width), f32),
            pltpu.VMEM((128, 32 * 128), jnp.bfloat16),
            pltpu.VMEM((96, 32 * 128), jnp.bfloat16),
            dma((chunks,)),
            dma((chunks,)),
        ],
        compiler_params=pltpu.CompilerParams(vmem_limit_bytes=24 * 2**20),
        name="wave",
    )(
        spectrum,
        sea_mask,
        courant,
        phase_speed,
        growth_rate,
        dissipation,
        intersection_tile,
        intersection_cell,
        intersection_weight,
        table,
        west,
        east,
    )

    roughness = pl.pallas_call(
        functools.partial(return_kernel, ranks),
        out_shape=jax.ShapeDtypeStruct((1,) + atmos_fields.shape[2:], f32),
        in_specs=[vmem],
        out_specs=vmem,
        scratch_shapes=[
            pltpu.VMEM((ATY, 8, 128), f32),
            dma((ATY,)),
            dma((ATY,)),
        ],
        compiler_params=pltpu.CompilerParams(collective_id=1, has_side_effects=True),
        name="give_back",
    )(stress)
    return (updated, roughness)


def solution(mesh):
    in_specs = (
        P(None, None, "groups", "gx"),
        P("groups", "gx"),
        P(),
        P(),
        P(),
        P(),
        P("gx", None, "groups", None),
        P(None, "groups", "gx"),
        P(None, "groups", "gx"),
        P(None, "groups", "gx"),
    )
    out_specs = (P(None, None, "groups", "gx"), P("gx", "groups", None))
    return jax.shard_map(
        functools.partial(on_device, mesh.shape["gx"]),
        mesh=mesh,
        in_specs=in_specs,
        out_specs=out_specs,
        check_vma=False,
    )
```

```python
import functools
import math

import jax
import jax.numpy as jnp
import numpy as np
from jax import lax
from jax.experimental import pallas as pl
from jax.experimental.pallas import tpu as pltpu
from jax.sharding import PartitionSpec as P

ATY = 4
FCHUNK = 6
MESH = pl.DeviceIdType.MESH


def directions(count):
    angles = np.arange(count, dtype=np.float32) * np.float32(2.0 * math.pi / count)
    cosine, sine = np.cos(angles), np.sin(angles)
    forward = [d for d in range(count) if cosine[d] >= 0]
    backward = [d for d in range(count) if cosine[d] < 0]
    return cosine, sine, forward, backward


def pack_constants(dirs, slots, chunks):
    cosine, sine, forward, backward = directions(dirs)
    table = np.zeros((2, 3, 8, 128), np.float32)
    for side, members in enumerate((forward, backward)):
        for c in range(chunks):
            for k, d in enumerate(members):
                lane = c * slots + 2 * k
                table[side, 0, :, lane : lane + 2] = abs(cosine[d])
                table[side, 1, :, lane : lane + 2] = max(sine[d], 0.0)
                table[side, 2, :, lane : lane + 2] = max(-sine[d], 0.0)
    return table


def lane_row(shape):
    lane = lax.broadcasted_iota(jnp.int32, shape, 1)
    row = lax.broadcasted_iota(jnp.int32, shape, 0)
    return lane, row


def exchange_kernel(
    ranks,
    spec_hbm,
    sea_ref,
    courant_ref,
    const_ref,
    atmos_ref,
    table_ref,
    west_ref,
    east_ref,
    spec,
    pack,
    in_sem,
    piece_send,
    piece_recv,
    halo_send,
    halo_recv,
):
    freqs, dirs = spec.shape[0], spec.shape[1]
    chunks = freqs // FCHUNK
    _, _, forward, backward = directions(dirs)
    slots = 2 * len(forward)
    me = lax.axis_index("gx")
    bands = ranks // ATY
    east, west = lax.rem(me + 1, ranks), lax.rem(me + ranks - 1, ranks)
    group, band = me // ATY, me // bands
    first_target = lax.rem(me, bands) * ATY
    own = lax.rem(me, bands) == group

    def load(g):
        span = pl.ds(g * FCHUNK, FCHUNK)
        return pltpu.make_async_copy(spec_hbm.at[span], spec.at[span], in_sem.at[g])

    for g in range(chunks):
        load(g).start()

    barrier = pltpu.get_barrier_semaphore()
    for device in (east, west):
        pl.semaphore_signal(barrier, inc=1, device_id={"gx": device}, device_id_type=MESH)
    for b in range(ATY):
        source = b * bands + group

        @pl.when(source != me)
        def _():
            pl.semaphore_signal(barrier, inc=1, device_id={"gx": source}, device_id_type=MESH)

    pl.semaphore_wait(barrier, 2 + ATY - own.astype(jnp.int32))

    span = atmos_ref.shape[3] // ATY

    def piece(j):
        return atmos_ref.at[0, :, :, pl.ds(j * span, span)]

    def piece_copy(j):
        return pltpu.make_async_remote_copy(
            src_ref=piece(j),
            dst_ref=table_ref.at[band],
            send_sem=piece_send.at[j],
            recv_sem=piece_recv.at[band],
            device_id={"gx": first_target + j},
            device_id_type=MESH,
        )

    for j in range(ATY):

        @pl.when(first_target + j != me)
        def _():
            piece_copy(j).start()

        @pl.when(first_target + j == me)
        def _():
            pltpu.make_async_copy(piece(j), table_ref.at[band], piece_recv.at[band]).start()

    lane, row = lane_row((8, 128))
    half = lane // 2
    odd = lane % 2 == 1
    sea = sea_ref[...].astype(jnp.float32)

    def tiled(shift):
        out = jnp.where(lane < 2, pltpu.roll(sea, shift, 1), 0.0)
        for step in (2, 4, 8, 16, 32, 64):
            out = out + pltpu.roll(out, step, 1)
        return out

    sea_pair = (tiled(2), tiled(0))
    freq_of_lane = lane // slots

    def chunk(c, acc):
        load(c).wait()
        acc = list(acc)
        for m in range(len(forward) + 1):
            for side, members, k in ((0, forward, m - 1), (1, backward, m)):
                if not 0 <= k < len(members):
                    continue
                here = half == c * (slots // 2) + k
                for fi in range(FCHUNK):
                    value = pltpu.roll(spec[c * FCHUNK + fi, members[k]], c * slots + 2 * m, 1)
                    at = side * FCHUNK + fi
                    acc[at] = jnp.where(here, value, acc[at])
        return tuple(acc)

    blank = jnp.zeros((8, 128), jnp.float32)
    acc = lax.fori_loop(0, chunks, chunk, (blank,) * (2 * FCHUNK))
    for fi in range(FCHUNK):
        speed = blank
        for c in range(chunks):
            speed = jnp.where(freq_of_lane == c, courant_ref[c * FCHUNK + fi], speed)
        for side in range(2):
            field = acc[side * FCHUNK + fi] * sea_pair[side]
            upwind = pltpu.roll(field, 1 if side == 0 else 127, 1)
            south = jnp.where(row == 0, 0.0, pltpu.roll(field, 1, 0))
            north = jnp.where(row == 7, 0.0, pltpu.roll(field, 7, 0))
            later = field - speed * const_ref[side, 0] * (field - upwind)
            later = later - speed * const_ref[side, 1] * (field - south)
            later = later - speed * const_ref[side, 2] * (field - north)
            later = later * sea_pair[side]
            if side == 0:
                both = jnp.where(odd, later, pltpu.roll(field, 127, 1))
            else:
                both = jnp.where(odd, pltpu.roll(field, 1, 1), later)
            pack[side, fi] = both

    to_east = pltpu.make_async_remote_copy(
        src_ref=pack.at[0],
        dst_ref=west_ref,
        send_sem=halo_send.at[0],
        recv_sem=halo_recv.at[0],
        device_id={"gx": east},
        device_id_type=MESH,
    )
    to_west = pltpu.make_async_remote_copy(
        src_ref=pack.at[1],
        dst_ref=east_ref,
        send_sem=halo_send.at[1],
        recv_sem=halo_recv.at[1],
        device_id={"gx": west},
        device_id_type=MESH,
    )
    to_east.start()
    to_west.start()

    for j in range(ATY):

        @pl.when(first_target + j != me)
        def _():
            piece_copy(j).wait_send()

    for b in range(ATY):
        pltpu.make_async_copy(table_ref.at[b], table_ref.at[b], piece_recv.at[b]).wait()
    to_east.wait()
    to_west.wait()


def wave_kernel(
    bands,
    spec_hbm,
    sea_ref,
    courant_ref,
    phase_ref,
    rate_ref,
    decay_ref,
    tile_ref,
    cell_ref,
    weight_ref,
    table_ref,
    west_ref,
    east_ref,
    out_hbm,
    stress_ref,
    spec,
    out,
    along_ref,
    lane_hot,
    row_hot,
    in_sem,
    out_sem,
):
    freqs, dirs = spec.shape[0], spec.shape[1]
    chunks = freqs // FCHUNK
    cosine, sine, forward, backward = directions(dirs)
    slots = 2 * len(forward)

    def load(g):
        span = pl.ds(g * FCHUNK, FCHUNK)
        return pltpu.make_async_copy(spec_hbm.at[span], spec.at[span], in_sem.at[g])

    def store(g):
        span = pl.ds(g * FCHUNK, FCHUNK)
        return pltpu.make_async_copy(out.at[span], out_hbm.at[span], out_sem.at[g])

    for g in range(chunks):
        load(g).start()

    lane, row = lane_row((8, 128))
    sea = sea_ref[...].astype(jnp.float32)

    tile = [tile_ref[l] for l in range(4)]
    cell = [cell_ref[l] for l in range(4)]
    weight = [weight_ref[l] for l in range(4)]
    low = [c & 127 for c in cell]
    high = []
    for l in range(4):
        band = jnp.zeros((8, 128), jnp.int32)
        for b in range(1, ATY):
            band = band + (tile[l] >= b * bands).astype(jnp.int32)
        high.append(band * 8 + (cell[l] >> 7))

    forcing = [[jnp.zeros((8, 128), jnp.float32) for _ in range(4)] for _ in range(4)]
    for h in range(32):
        b, r, c = h // 8, h % 8 // 2, h % 2
        hit = [high[l] == h for l in range(4)]
        for k in range(4):
            line = jnp.broadcast_to(table_ref[b, k, pl.ds(r, 1), pl.ds(c * 128, 128)], (8, 128))
            for l in range(4):
                found = jnp.take_along_axis(line, low[l], axis=1)
                forcing[k][l] = jnp.where(hit[l], found, forcing[k][l])
    east_wind, north_wind, air, stability = [
        (weight[0] * v[0] + weight[1] * v[1]) + (weight[2] * v[2] + weight[3] * v[3])
        for v in forcing
    ]
    for d in range(dirs):
        along_ref[d] = float(cosine[d]) * east_wind + float(sine[d]) * north_wind

    lows = lax.broadcasted_iota(jnp.int32, (128, 128), 0)
    for l in range(4):
        for y in range(8):
            at = pl.ds((l * 8 + y) * 128, 128)
            same = lows == jnp.broadcast_to(low[l][y : y + 1], (128, 128))
            lane_hot[:, at] = jnp.where(same, 1.0, 0.0).astype(jnp.bfloat16)

    first, last = lane == 0, lane == 127
    bottom, top = row == 0, row == 7

    def propagate(c, energy):
        load(c).wait()
        sums = [energy] + [jnp.zeros((8, 128), jnp.float32) for _ in range(3)]
        speeds = [courant_ref[c * FCHUNK + fi] for fi in range(FCHUNK)]
        for k in range(max(len(forward), len(backward))):
            for side, members in enumerate((forward, backward)):
                if k >= len(members):
                    continue
                d = members[k]
                halo_ref = (west_ref, east_ref)[side]
                turn = 127 - 2 * k - c * slots
                halos = [pltpu.roll(halo_ref[fi], turn, 1) for fi in range(FCHUNK)]
                shift = 1 if side == 0 else 127
                done = []
                for fi in range(FCHUNK):
                    step_x = speeds[fi] * float(abs(cosine[d]))
                    step_y = speeds[fi] * float(abs(sine[d]))
                    keep = 1.0 - step_x - step_y
                    field = spec[c * FCHUNK + fi, d] * sea
                    for substep in range(2):
                        if substep == 0:
                            upwind = jnp.where(last if side == 0 else first, halos[fi], field)
                            upwind = pltpu.roll(upwind, shift, 1)
                        else:
                            upwind = pltpu.roll(field, shift, 1)
                            upwind = jnp.where(first if side == 0 else last, halos[fi], upwind)
                        result = keep * field + step_x * upwind
                        if sine[d] != 0:
                            up = sine[d] > 0
                            beside = pltpu.roll(field, 1 if up else 7, 0)
                            beside = jnp.where(bottom if up else top, 0.0, beside)
                            result = result + step_y * beside
                        field = sea * result
                    done.append(field)
                for fi, field in enumerate(done):
                    out[c * FCHUNK + fi, d] = field
                    sums[fi % 4] = sums[fi % 4] + field
        return (sums[0] + sums[1]) + (sums[2] + sums[3])

    energy = lax.fori_loop(0, chunks, propagate, jnp.zeros((8, 128), jnp.float32))

    base = air * jnp.exp(0.3 * stability)

    def sources(g, stress):
        sums = [stress] + [jnp.zeros((8, 128), jnp.float32) for _ in range(3)]
        for fi in range(FCHUNK):
            f = g * FCHUNK + fi
            offset = rate_ref[f] * base
            slope = offset / phase_ref[f]
            scale = 1.0 / (1.0 + decay_ref[f] * energy)
            for d in range(dirs):
                growth = jnp.maximum(along_ref[d] * slope - offset, 0.0)
                scaled = out[f, d] * scale
                updated = scaled + scaled * growth
                out[f, d] = updated
                sums[d % 4] = sums[d % 4] + growth * updated
        store(g).start()
        return (sums[0] + sums[1]) + (sums[2] + sums[3])

    stress = lax.fori_loop(0, chunks, sources, jnp.zeros((8, 128), jnp.float32))

    surface = sea * (0.01 * (east_wind * east_wind + north_wind * north_wind + stress))
    highs = lax.broadcasted_iota(jnp.int32, (32, 128), 0)
    for l in range(4):
        rest = weight[l] * surface
        parts = []
        for _ in range(3):
            part = rest.astype(jnp.bfloat16).astype(jnp.float32)
            parts.append(part)
            rest = rest - part
        for y in range(8):
            at = pl.ds((l * 8 + y) * 128, 128)
            same = highs == jnp.broadcast_to(high[l][y : y + 1], (32, 128))
            for p, part in enumerate(parts):
                line = jnp.broadcast_to(part[y : y + 1], (32, 128))
                row_hot[pl.ds(p * 32, 32), at] = jnp.where(same, line, 0.0).astype(jnp.bfloat16)
    spread = lax.dot_general(
        row_hot[...],
        lane_hot[...],
        (((1,), (1,)), ((), ())),
        preferred_element_type=jnp.float32,
    )
    stress_ref[...] = spread[0:32] + (spread[32:64] + spread[64:96])

    for g in range(chunks):
        store(g).wait()


def return_kernel(ranks, stress_ref, out_ref, landed, send_sem, recv_sem):
    me = lax.axis_index("gx")
    bands = ranks // ATY
    group = me // ATY
    slot = lax.rem(me, ATY)
    first_source = lax.rem(me, bands) * ATY
    own = lax.rem(me, bands) == group
    barrier = pltpu.get_barrier_semaphore()
    for j in range(ATY):

        @pl.when(first_source + j != me)
        def _():
            pl.semaphore_signal(
                barrier, inc=1, device_id={"gx": first_source + j}, device_id_type=MESH
            )

    pl.semaphore_wait(barrier, ATY - own.astype(jnp.int32))

    def piece(b):
        return stress_ref.at[pl.ds(b * 8, 8)]

    def piece_copy(b):
        return pltpu.make_async_remote_copy(
            src_ref=piece(b),
            dst_ref=landed.at[slot],
            send_sem=send_sem.at[b],
            recv_sem=recv_sem.at[slot],
            device_id={"gx": b * bands + group},
            device_id_type=MESH,
        )

    for b in range(ATY):

        @pl.when(b * bands + group != me)
        def _():
            piece_copy(b).start()

        @pl.when(b * bands + group == me)
        def _():
            pltpu.make_async_copy(piece(b), landed.at[slot], recv_sem.at[slot]).start()

    for j in range(ATY):
        pltpu.make_async_copy(landed.at[j], landed.at[j], recv_sem.at[j]).wait()
        for r in range(4):
            for c in range(2):
                out_ref[0, pl.ds(r, 1), pl.ds(j * 256 + c * 128, 128)] = landed[
                    j, pl.ds(2 * r + c, 1), :
                ]
    for b in range(ATY):

        @pl.when(b * bands + group != me)
        def _():
            piece_copy(b).wait_send()


def on_device(
    ranks,
    spectrum,
    sea_mask,
    courant,
    phase_speed,
    growth_rate,
    dissipation,
    atmos_fields,
    intersection_tile,
    intersection_cell,
    intersection_weight,
):
    freqs, dirs, lat, width = spectrum.shape
    chunks = freqs // FCHUNK
    bands = ranks // ATY
    f32 = jnp.float32
    _, _, forward, _ = directions(dirs)
    consts = jnp.asarray(pack_constants(dirs, 2 * len(forward), chunks))
    anywhere = pl.BlockSpec(memory_space=pltpu.HBM)
    vmem = pl.BlockSpec(memory_space=pltpu.VMEM)
    smem = pl.BlockSpec(memory_space=pltpu.SMEM)
    dma = pltpu.SemaphoreType.DMA
    span = atmos_fields.shape[3] // ATY
    halo = jax.ShapeDtypeStruct((FCHUNK, lat, width), f32)
    table, west, east = pl.pallas_call(
        functools.partial(exchange_kernel, ranks),
        out_shape=(
            jax.ShapeDtypeStruct((ATY,) + atmos_fields.shape[1:3] + (span,), f32),
            halo,
            halo,
        ),
        in_specs=[anywhere, vmem, smem, vmem, anywhere],
        out_specs=(anywhere, anywhere, anywhere),
        scratch_shapes=[
            pltpu.VMEM(spectrum.shape, f32),
            pltpu.VMEM((2, FCHUNK, lat, width), f32),
            dma((chunks,)),
            dma((ATY,)),
            dma((ATY,)),
            dma((2,)),
            dma((2,)),
        ],
        compiler_params=pltpu.CompilerParams(
            collective_id=0, has_side_effects=True, vmem_limit_bytes=62 * 2**20
        ),
        name="exchange",
    )(spectrum, sea_mask, courant, consts, atmos_fields)

    updated, stress = pl.pallas_call(
        functools.partial(wave_kernel, bands),
        out_shape=(
            jax.ShapeDtypeStruct(spectrum.shape, f32),
            jax.ShapeDtypeStruct((32, 128), f32),
        ),
        in_specs=[anywhere, vmem, smem, smem, smem, smem] + [vmem] * 6,
        out_specs=(anywhere, vmem),
        scratch_shapes=[
            pltpu.VMEM(spectrum.shape, f32),
            pltpu.VMEM(spectrum.shape, f32),
            pltpu.VMEM((dirs, lat, width), f32),
            pltpu.VMEM((128, 32 * 128), jnp.bfloat16),
            pltpu.VMEM((96, 32 * 128), jnp.bfloat16),
            dma((chunks,)),
            dma((chunks,)),
        ],
        compiler_params=pltpu.CompilerParams(vmem_limit_bytes=62 * 2**20),
        name="wave",
    )(
        spectrum,
        sea_mask,
        courant,
        phase_speed,
        growth_rate,
        dissipation,
        intersection_tile,
        intersection_cell,
        intersection_weight,
        table,
        west,
        east,
    )

    roughness = pl.pallas_call(
        functools.partial(return_kernel, ranks),
        out_shape=jax.ShapeDtypeStruct((1,) + atmos_fields.shape[2:], f32),
        in_specs=[vmem],
        out_specs=vmem,
        scratch_shapes=[
            pltpu.VMEM((ATY, 8, 128), f32),
            dma((ATY,)),
            dma((ATY,)),
        ],
        compiler_params=pltpu.CompilerParams(collective_id=1, has_side_effects=True, vmem_limit_bytes=62 * 2**20),
        name="give_back",
    )(stress)
    return (updated, roughness)


def solution(mesh):
    in_specs = (
        P(None, None, "groups", "gx"),
        P("groups", "gx"),
        P(),
        P(),
        P(),
        P(),
        P("gx", None, "groups", None),
        P(None, "groups", "gx"),
        P(None, "groups", "gx"),
        P(None, "groups", "gx"),
    )
    out_specs = (P(None, None, "groups", "gx"), P("gx", "groups", None))
    return jax.shard_map(
        functools.partial(on_device, mesh.shape["gx"]),
        mesh=mesh,
        in_specs=in_specs,
        out_specs=out_specs,
        check_vma=False,
    )
```

```python
import functools
import math

import jax
import jax.numpy as jnp
import numpy as np
from jax import lax
from jax.experimental import pallas as pl
from jax.experimental.pallas import tpu as pltpu
from jax.sharding import PartitionSpec as P

ATY = 4
FCHUNK = 6
MESH = pl.DeviceIdType.MESH


def directions(count):
    angles = np.arange(count, dtype=np.float32) * np.float32(2.0 * math.pi / count)
    cosine, sine = np.cos(angles), np.sin(angles)
    forward = [d for d in range(count) if cosine[d] >= 0]
    backward = [d for d in range(count) if cosine[d] < 0]
    return cosine, sine, forward, backward


def pack_constants(dirs, slots, chunks):
    cosine, sine, forward, backward = directions(dirs)
    table = np.zeros((2, 3, 8, 128), np.float32)
    for side, members in enumerate((forward, backward)):
        for c in range(chunks):
            for k, d in enumerate(members):
                lane = c * slots + 2 * k
                table[side, 0, :, lane : lane + 2] = abs(cosine[d])
                table[side, 1, :, lane : lane + 2] = max(sine[d], 0.0)
                table[side, 2, :, lane : lane + 2] = max(-sine[d], 0.0)
    return table


def lane_row(shape):
    lane = lax.broadcasted_iota(jnp.int32, shape, 1)
    row = lax.broadcasted_iota(jnp.int32, shape, 0)
    return lane, row


def exchange_kernel(
    ranks,
    spec_hbm,
    sea_ref,
    courant_ref,
    const_ref,
    atmos_ref,
    table_ref,
    west_ref,
    east_ref,
    spec,
    stage,
    pack,
    in_sem,
    piece_send,
    piece_recv,
    halo_send,
    halo_recv,
):
    freqs, dirs = spec.shape[0], spec.shape[1]
    chunks = freqs // FCHUNK
    _, _, forward, backward = directions(dirs)
    slots = 2 * len(forward)
    me = lax.axis_index("gx")
    bands = ranks // ATY
    east, west = lax.rem(me + 1, ranks), lax.rem(me + ranks - 1, ranks)
    group, band = me // ATY, me // bands
    first_target = lax.rem(me, bands) * ATY
    own = lax.rem(me, bands) == group

    def load(g):
        span = pl.ds(g * FCHUNK, FCHUNK)
        return pltpu.make_async_copy(spec_hbm.at[span], spec.at[span], in_sem.at[g])

    for g in range(chunks):
        load(g).start()

    barrier = pltpu.get_barrier_semaphore()
    for device in (east, west):
        pl.semaphore_signal(barrier, inc=1, device_id={"gx": device}, device_id_type=MESH)
    for b in range(ATY):
        source = b * bands + group

        @pl.when(source != me)
        def _():
            pl.semaphore_signal(barrier, inc=1, device_id={"gx": source}, device_id_type=MESH)

    pl.semaphore_wait(barrier, 2 + ATY - own.astype(jnp.int32))

    span = atmos_ref.shape[3] // ATY

    def piece(j):
        return atmos_ref.at[0, :, :, pl.ds(j * span, span)]

    def piece_copy(j):
        return pltpu.make_async_remote_copy(
            src_ref=piece(j),
            dst_ref=table_ref.at[band],
            send_sem=piece_send.at[j],
            recv_sem=piece_recv.at[band],
            device_id={"gx": first_target + j},
            device_id_type=MESH,
        )

    for j in range(ATY):

        @pl.when(first_target + j != me)
        def _():
            piece_copy(j).start()

        @pl.when(first_target + j == me)
        def _():
            pltpu.make_async_copy(piece(j), table_ref.at[band], piece_recv.at[band]).start()

    lane, row = lane_row((8, 128))
    half = lane // 2
    odd = lane % 2 == 1
    sea = sea_ref[...].astype(jnp.float32)

    def tiled(shift):
        out = jnp.where(lane < 2, pltpu.roll(sea, shift, 1), 0.0)
        for step in (2, 4, 8, 16, 32, 64):
            out = out + pltpu.roll(out, step, 1)
        return out

    sea_pair = (tiled(2), tiled(0))
    freq_of_lane = lane // slots

    blank = jnp.zeros((8, 128), jnp.float32)
    for c in range(chunks):
        load(c).wait()
    for m in range(len(forward) + 1):
        for side, members, k in ((0, forward, m - 1), (1, backward, m)):
            if not 0 <= k < len(members):
                continue
            here = half == k
            for c in range(chunks):
                merged = []
                for fi in range(FCHUNK):
                    value = spec[c * FCHUNK + fi, members[k]]
                    if m:
                        value = pltpu.roll(value, 2 * m, 1)
                    before = blank if k == 0 else stage[side, c * FCHUNK + fi]
                    merged.append(jnp.where(here, value, before))
                for fi in range(FCHUNK):
                    stage[side, c * FCHUNK + fi] = merged[fi]
    acc = [stage[n // FCHUNK, n % FCHUNK] for n in range(2 * FCHUNK)]
    for c in range(1, chunks):
        for n in range(2 * FCHUNK):
            value = stage[n // FCHUNK, c * FCHUNK + n % FCHUNK]
            acc[n] = acc[n] + pltpu.roll(value, c * slots, 1)
    for fi in range(FCHUNK):
        speed = blank
        for c in range(chunks):
            speed = jnp.where(freq_of_lane == c, courant_ref[c * FCHUNK + fi], speed)
        for side in range(2):
            field = acc[side * FCHUNK + fi] * sea_pair[side]
            upwind = pltpu.roll(field, 1 if side == 0 else 127, 1)
            south = jnp.where(row == 0, 0.0, pltpu.roll(field, 1, 0))
            north = jnp.where(row == 7, 0.0, pltpu.roll(field, 7, 0))
            later = field - speed * const_ref[side, 0] * (field - upwind)
            later = later - speed * const_ref[side, 1] * (field - south)
            later = later - speed * const_ref[side, 2] * (field - north)
            later = later * sea_pair[side]
            if side == 0:
                both = jnp.where(odd, later, pltpu.roll(field, 127, 1))
            else:
                both = jnp.where(odd, pltpu.roll(field, 1, 1), later)
            pack[side, fi] = both

    to_east = pltpu.make_async_remote_copy(
        src_ref=pack.at[0],
        dst_ref=west_ref,
        send_sem=halo_send.at[0],
        recv_sem=halo_recv.at[0],
        device_id={"gx": east},
        device_id_type=MESH,
    )
    to_west = pltpu.make_async_remote_copy(
        src_ref=pack.at[1],
        dst_ref=east_ref,
        send_sem=halo_send.at[1],
        recv_sem=halo_recv.at[1],
        device_id={"gx": west},
        device_id_type=MESH,
    )
    to_east.start()
    to_west.start()

    for j in range(ATY):

        @pl.when(first_target + j != me)
        def _():
            piece_copy(j).wait_send()

    for b in range(ATY):
        pltpu.make_async_copy(table_ref.at[b], table_ref.at[b], piece_recv.at[b]).wait()
    to_east.wait()
    to_west.wait()


def wave_kernel(
    bands,
    spec_hbm,
    sea_ref,
    courant_ref,
    phase_ref,
    rate_ref,
    decay_ref,
    tile_ref,
    cell_ref,
    weight_ref,
    table_ref,
    west_ref,
    east_ref,
    out_hbm,
    stress_ref,
    spec,
    out,
    stage,
    along_ref,
    lane_hot,
    row_hot,
    in_sem,
    out_sem,
):
    freqs, dirs = spec.shape[0], spec.shape[1]
    chunks = freqs // FCHUNK
    cosine, sine, forward, backward = directions(dirs)
    slots = 2 * len(forward)

    def load(g):
        span = pl.ds(g * FCHUNK, FCHUNK)
        return pltpu.make_async_copy(spec_hbm.at[span], spec.at[span], in_sem.at[g])

    def store(g):
        span = pl.ds(g * FCHUNK, FCHUNK)
        return pltpu.make_async_copy(out.at[span], out_hbm.at[span], out_sem.at[g])

    for g in range(chunks):
        load(g).start()

    lane, row = lane_row((8, 128))
    sea = sea_ref[...].astype(jnp.float32)

    tile = [tile_ref[l] for l in range(4)]
    cell = [cell_ref[l] for l in range(4)]
    weight = [weight_ref[l] for l in range(4)]
    low = [c & 127 for c in cell]
    high = []
    for l in range(4):
        band = jnp.zeros((8, 128), jnp.int32)
        for b in range(1, ATY):
            band = band + (tile[l] >= b * bands).astype(jnp.int32)
        high.append(band * 8 + (cell[l] >> 7))

    forcing = [[jnp.zeros((8, 128), jnp.float32) for _ in range(4)] for _ in range(4)]
    for h in range(32):
        b, r, c = h // 8, h % 8 // 2, h % 2
        hit = [high[l] == h for l in range(4)]
        for k in range(4):
            line = jnp.broadcast_to(table_ref[b, k, pl.ds(r, 1), pl.ds(c * 128, 128)], (8, 128))
            for l in range(4):
                found = jnp.take_along_axis(line, low[l], axis=1)
                forcing[k][l] = jnp.where(hit[l], found, forcing[k][l])
    east_wind, north_wind, air, stability = [
        (weight[0] * v[0] + weight[1] * v[1]) + (weight[2] * v[2] + weight[3] * v[3])
        for v in forcing
    ]
    for d in range(dirs):
        along_ref[d] = float(cosine[d]) * east_wind + float(sine[d]) * north_wind

    lows = lax.broadcasted_iota(jnp.int32, (128, 128), 0)
    for l in range(4):
        for y in range(8):
            at = pl.ds((l * 8 + y) * 128, 128)
            same = lows == jnp.broadcast_to(low[l][y : y + 1], (128, 128))
            lane_hot[:, at] = jnp.where(same, 1.0, 0.0).astype(jnp.bfloat16)

    first, last = lane == 0, lane == 127
    bottom, top = row == 0, row == 7

    sides = ((forward, west_ref), (backward, east_ref))
    for c in range(chunks):
        for side in range(2):
            for fi in range(FCHUNK):
                halo = sides[side][1][fi]
                if c:
                    halo = pltpu.roll(halo, 128 - c * slots, 1)
                stage[side, c * FCHUNK + fi] = halo
    for k in range(len(forward)):
        for side in range(2):
            members = sides[side][0]
            if k >= len(members):
                continue
            for c in range(chunks):
                rolled = [
                    pltpu.roll(stage[side, c * FCHUNK + fi], 127 - 2 * k, 1)
                    for fi in range(FCHUNK)
                ]
                for fi in range(FCHUNK):
                    out[c * FCHUNK + fi, members[k]] = rolled[fi]

    def propagate(c, energy):
        load(c).wait()
        sums = [energy] + [jnp.zeros((8, 128), jnp.float32) for _ in range(3)]
        speeds = [courant_ref[c * FCHUNK + fi] for fi in range(FCHUNK)]
        for side, members in enumerate((forward, backward)):
            shift = 1 if side == 0 else 127
            for d in members:
                done = []
                for fi in range(FCHUNK):
                    step_x = speeds[fi] * float(abs(cosine[d]))
                    step_y = speeds[fi] * float(abs(sine[d]))
                    keep = 1.0 - step_x - step_y
                    halo = out[c * FCHUNK + fi, d]
                    field = spec[c * FCHUNK + fi, d] * sea
                    for substep in range(2):
                        if substep == 0:
                            upwind = jnp.where(last if side == 0 else first, halo, field)
                            upwind = pltpu.roll(upwind, shift, 1)
                        else:
                            upwind = pltpu.roll(field, shift, 1)
                            upwind = jnp.where(first if side == 0 else last, halo, upwind)
                        result = keep * field + step_x * upwind
                        if sine[d] != 0:
                            up = sine[d] > 0
                            beside = pltpu.roll(field, 1 if up else 7, 0)
                            beside = jnp.where(bottom if up else top, 0.0, beside)
                            result = result + step_y * beside
                        field = sea * result
                    done.append(field)
                for fi, field in enumerate(done):
                    out[c * FCHUNK + fi, d] = field
                    sums[fi % 4] = sums[fi % 4] + field
        return (sums[0] + sums[1]) + (sums[2] + sums[3])

    energy = lax.fori_loop(0, chunks, propagate, jnp.zeros((8, 128), jnp.float32))

    base = air * jnp.exp(0.3 * stability)

    def sources(g, stress):
        sums = [stress] + [jnp.zeros((8, 128), jnp.float32) for _ in range(3)]
        for fi in range(FCHUNK):
            f = g * FCHUNK + fi
            offset = rate_ref[f] * base
            slope = offset / phase_ref[f]
            scale = 1.0 / (1.0 + decay_ref[f] * energy)
            for d in range(dirs):
                growth = jnp.maximum(along_ref[d] * slope - offset, 0.0)
                scaled = out[f, d] * scale
                updated = scaled + scaled * growth
                out[f, d] = updated
                sums[d % 4] = sums[d % 4] + growth * updated
        store(g).start()
        return (sums[0] + sums[1]) + (sums[2] + sums[3])

    stress = lax.fori_loop(0, chunks, sources, jnp.zeros((8, 128), jnp.float32))

    surface = sea * (0.01 * (east_wind * east_wind + north_wind * north_wind + stress))
    highs = lax.broadcasted_iota(jnp.int32, (32, 128), 0)
    for l in range(4):
        rest = weight[l] * surface
        parts = []
        for _ in range(3):
            part = rest.astype(jnp.bfloat16).astype(jnp.float32)
            parts.append(part)
            rest = rest - part
        for y in range(8):
            at = pl.ds((l * 8 + y) * 128, 128)
            same = highs == jnp.broadcast_to(high[l][y : y + 1], (32, 128))
            for p, part in enumerate(parts):
                line = jnp.broadcast_to(part[y : y + 1], (32, 128))
                row_hot[pl.ds(p * 32, 32), at] = jnp.where(same, line, 0.0).astype(jnp.bfloat16)
    spread = lax.dot_general(
        row_hot[...],
        lane_hot[...],
        (((1,), (1,)), ((), ())),
        preferred_element_type=jnp.float32,
    )
    stress_ref[...] = spread[0:32] + (spread[32:64] + spread[64:96])

    for g in range(chunks):
        store(g).wait()


def return_kernel(ranks, stress_ref, out_ref, landed, send_sem, recv_sem):
    me = lax.axis_index("gx")
    bands = ranks // ATY
    group = me // ATY
    slot = lax.rem(me, ATY)
    first_source = lax.rem(me, bands) * ATY
    own = lax.rem(me, bands) == group
    barrier = pltpu.get_barrier_semaphore()
    for j in range(ATY):

        @pl.when(first_source + j != me)
        def _():
            pl.semaphore_signal(
                barrier, inc=1, device_id={"gx": first_source + j}, device_id_type=MESH
            )

    pl.semaphore_wait(barrier, ATY - own.astype(jnp.int32))

    def piece(b):
        return stress_ref.at[pl.ds(b * 8, 8)]

    def piece_copy(b):
        return pltpu.make_async_remote_copy(
            src_ref=piece(b),
            dst_ref=landed.at[slot],
            send_sem=send_sem.at[b],
            recv_sem=recv_sem.at[slot],
            device_id={"gx": b * bands + group},
            device_id_type=MESH,
        )

    for b in range(ATY):

        @pl.when(b * bands + group != me)
        def _():
            piece_copy(b).start()

        @pl.when(b * bands + group == me)
        def _():
            pltpu.make_async_copy(piece(b), landed.at[slot], recv_sem.at[slot]).start()

    for j in range(ATY):
        pltpu.make_async_copy(landed.at[j], landed.at[j], recv_sem.at[j]).wait()
        for r in range(4):
            for c in range(2):
                out_ref[0, pl.ds(r, 1), pl.ds(j * 256 + c * 128, 128)] = landed[
                    j, pl.ds(2 * r + c, 1), :
                ]
    for b in range(ATY):

        @pl.when(b * bands + group != me)
        def _():
            piece_copy(b).wait_send()


def on_device(
    ranks,
    spectrum,
    sea_mask,
    courant,
    phase_speed,
    growth_rate,
    dissipation,
    atmos_fields,
    intersection_tile,
    intersection_cell,
    intersection_weight,
):
    freqs, dirs, lat, width = spectrum.shape
    chunks = freqs // FCHUNK
    bands = ranks // ATY
    f32 = jnp.float32
    _, _, forward, _ = directions(dirs)
    consts = jnp.asarray(pack_constants(dirs, 2 * len(forward), chunks))
    anywhere = pl.BlockSpec(memory_space=pltpu.HBM)
    vmem = pl.BlockSpec(memory_space=pltpu.VMEM)
    smem = pl.BlockSpec(memory_space=pltpu.SMEM)
    dma = pltpu.SemaphoreType.DMA
    span = atmos_fields.shape[3] // ATY
    halo = jax.ShapeDtypeStruct((FCHUNK, lat, width), f32)
    table, west, east = pl.pallas_call(
        functools.partial(exchange_kernel, ranks),
        out_shape=(
            jax.ShapeDtypeStruct((ATY,) + atmos_fields.shape[1:3] + (span,), f32),
            halo,
            halo,
        ),
        in_specs=[anywhere, vmem, smem, vmem, anywhere],
        out_specs=(anywhere, anywhere, anywhere),
        scratch_shapes=[
            pltpu.VMEM(spectrum.shape, f32),
            pltpu.VMEM((2, freqs, lat, width), f32),
            pltpu.VMEM((2, FCHUNK, lat, width), f32),
            dma((chunks,)),
            dma((ATY,)),
            dma((ATY,)),
            dma((2,)),
            dma((2,)),
        ],
        compiler_params=pltpu.CompilerParams(
            collective_id=0, has_side_effects=True, vmem_limit_bytes=62 * 2**20
        ),
        name="exchange",
    )(spectrum, sea_mask, courant, consts, atmos_fields)

    updated, stress = pl.pallas_call(
        functools.partial(wave_kernel, bands),
        out_shape=(
            jax.ShapeDtypeStruct(spectrum.shape, f32),
            jax.ShapeDtypeStruct((32, 128), f32),
        ),
        in_specs=[anywhere, vmem, smem, smem, smem, smem] + [vmem] * 6,
        out_specs=(anywhere, vmem),
        scratch_shapes=[
            pltpu.VMEM(spectrum.shape, f32),
            pltpu.VMEM(spectrum.shape, f32),
            pltpu.VMEM((2, freqs, lat, width), f32),
            pltpu.VMEM((dirs, lat, width), f32),
            pltpu.VMEM((128, 32 * 128), jnp.bfloat16),
            pltpu.VMEM((96, 32 * 128), jnp.bfloat16),
            dma((chunks,)),
            dma((chunks,)),
        ],
        compiler_params=pltpu.CompilerParams(vmem_limit_bytes=62 * 2**20),
        name="wave",
    )(
        spectrum,
        sea_mask,
        courant,
        phase_speed,
        growth_rate,
        dissipation,
        intersection_tile,
        intersection_cell,
        intersection_weight,
        table,
        west,
        east,
    )

    roughness = pl.pallas_call(
        functools.partial(return_kernel, ranks),
        out_shape=jax.ShapeDtypeStruct((1,) + atmos_fields.shape[2:], f32),
        in_specs=[anywhere],
        out_specs=vmem,
        scratch_shapes=[
            pltpu.VMEM((ATY, 8, 128), f32),
            dma((ATY,)),
            dma((ATY,)),
        ],
        compiler_params=pltpu.CompilerParams(collective_id=1, has_side_effects=True, vmem_limit_bytes=62 * 2**20),
        name="give_back",
    )(stress)
    return (updated, roughness)


def solution(mesh):
    in_specs = (
        P(None, None, "groups", "gx"),
        P("groups", "gx"),
        P(),
        P(),
        P(),
        P(),
        P("gx", None, "groups", None),
        P(None, "groups", "gx"),
        P(None, "groups", "gx"),
        P(None, "groups", "gx"),
    )
    out_specs = (P(None, None, "groups", "gx"), P("gx", "groups", None))
    return jax.shard_map(
        functools.partial(on_device, mesh.shape["gx"]),
        mesh=mesh,
        in_specs=in_specs,
        out_specs=out_specs,
        check_vma=False,
    )
```

```python
import functools
import math

import jax
import jax.numpy as jnp
import numpy as np
from jax import lax
from jax.experimental import pallas as pl
from jax.experimental.pallas import tpu as pltpu
from jax.sharding import PartitionSpec as P

ATY = 4
FCHUNK = 6
MESH = pl.DeviceIdType.MESH


def directions(count):
    angles = np.arange(count, dtype=np.float32) * np.float32(2.0 * math.pi / count)
    cosine, sine = np.cos(angles), np.sin(angles)
    forward = [d for d in range(count) if cosine[d] >= 0]
    backward = [d for d in range(count) if cosine[d] < 0]
    return cosine, sine, forward, backward


def pack_constants(dirs, slots, chunks):
    cosine, sine, forward, backward = directions(dirs)
    table = np.zeros((2, 3, 8, 128), np.float32)
    for side, members in enumerate((forward, backward)):
        for c in range(chunks):
            for k, d in enumerate(members):
                lane = c * slots + 2 * k
                table[side, 0, :, lane : lane + 2] = abs(cosine[d])
                table[side, 1, :, lane : lane + 2] = max(sine[d], 0.0)
                table[side, 2, :, lane : lane + 2] = max(-sine[d], 0.0)
    return table


def lane_row(shape):
    lane = lax.broadcasted_iota(jnp.int32, shape, 1)
    row = lax.broadcasted_iota(jnp.int32, shape, 0)
    return lane, row


def exchange_kernel(
    ranks,
    spec_hbm,
    sea_ref,
    courant_ref,
    const_ref,
    atmos_ref,
    table_ref,
    west_ref,
    east_ref,
    spec,
    stage,
    pack,
    in_sem,
    piece_send,
    piece_recv,
    halo_send,
    halo_recv,
):
    freqs, dirs = spec.shape[0], spec.shape[1]
    chunks = freqs // FCHUNK
    _, _, forward, backward = directions(dirs)
    slots = 2 * len(forward)
    me = lax.axis_index("gx")
    bands = ranks // ATY
    east, west = lax.rem(me + 1, ranks), lax.rem(me + ranks - 1, ranks)
    group, band = me // ATY, me // bands
    first_target = lax.rem(me, bands) * ATY
    own = lax.rem(me, bands) == group

    def load(g):
        span = pl.ds(g * FCHUNK, FCHUNK)
        return pltpu.make_async_copy(spec_hbm.at[span], spec.at[span], in_sem.at[g])

    for g in range(chunks):
        load(g).start()

    barrier = pltpu.get_barrier_semaphore()
    for device in (east, west):
        pl.semaphore_signal(barrier, inc=1, device_id={"gx": device}, device_id_type=MESH)
    for b in range(ATY):
        source = b * bands + group

        @pl.when(source != me)
        def _():
            pl.semaphore_signal(barrier, inc=1, device_id={"gx": source}, device_id_type=MESH)

    span = atmos_ref.shape[3] // ATY

    def piece(j):
        return atmos_ref.at[0, :, :, pl.ds(j * span, span)]

    def piece_copy(j):
        return pltpu.make_async_remote_copy(
            src_ref=piece(j),
            dst_ref=table_ref.at[band],
            send_sem=piece_send.at[j],
            recv_sem=piece_recv.at[band],
            device_id={"gx": first_target + j},
            device_id_type=MESH,
        )

    def send_pieces():
        pl.semaphore_wait(barrier, 2 + ATY - own.astype(jnp.int32))

        for j in range(ATY):

            @pl.when(first_target + j != me)
            def _():
                piece_copy(j).start()

            @pl.when(first_target + j == me)
            def _():
                pltpu.make_async_copy(piece(j), table_ref.at[band], piece_recv.at[band]).start()

    lane, row = lane_row((8, 128))
    half = lane // 2
    odd = lane % 2 == 1
    sea = sea_ref[...].astype(jnp.float32)

    def tiled(shift):
        out = jnp.where(lane < 2, pltpu.roll(sea, shift, 1), 0.0)
        for step in (2, 4, 8, 16, 32, 64):
            out = out + pltpu.roll(out, step, 1)
        return out

    sea_pair = (tiled(2), tiled(0))
    freq_of_lane = lane // slots

    blank = jnp.zeros((8, 128), jnp.float32)
    for c in range(chunks):
        load(c).wait()
    for m in range(len(forward) + 1):
        if m == len(forward) // 2:
            send_pieces()
        for side, members, k in ((0, forward, m - 1), (1, backward, m)):
            if not 0 <= k < len(members):
                continue
            here = half == k
            for c in range(chunks):
                merged = []
                for fi in range(FCHUNK):
                    value = spec[c * FCHUNK + fi, members[k]]
                    if m:
                        value = pltpu.roll(value, 2 * m, 1)
                    before = blank if k == 0 else stage[side, c * FCHUNK + fi]
                    merged.append(jnp.where(here, value, before))
                for fi in range(FCHUNK):
                    stage[side, c * FCHUNK + fi] = merged[fi]
    acc = [stage[n // FCHUNK, n % FCHUNK] for n in range(2 * FCHUNK)]
    for c in range(1, chunks):
        for n in range(2 * FCHUNK):
            value = stage[n // FCHUNK, c * FCHUNK + n % FCHUNK]
            acc[n] = acc[n] + pltpu.roll(value, c * slots, 1)
    for fi in range(FCHUNK):
        speed = blank
        for c in range(chunks):
            speed = jnp.where(freq_of_lane == c, courant_ref[c * FCHUNK + fi], speed)
        for side in range(2):
            field = acc[side * FCHUNK + fi] * sea_pair[side]
            upwind = pltpu.roll(field, 1 if side == 0 else 127, 1)
            south = jnp.where(row == 0, 0.0, pltpu.roll(field, 1, 0))
            north = jnp.where(row == 7, 0.0, pltpu.roll(field, 7, 0))
            later = field - speed * const_ref[side, 0] * (field - upwind)
            later = later - speed * const_ref[side, 1] * (field - south)
            later = later - speed * const_ref[side, 2] * (field - north)
            later = later * sea_pair[side]
            if side == 0:
                both = jnp.where(odd, later, pltpu.roll(field, 127, 1))
            else:
                both = jnp.where(odd, pltpu.roll(field, 1, 1), later)
            pack[side, fi] = both

    to_east = pltpu.make_async_remote_copy(
        src_ref=pack.at[0],
        dst_ref=west_ref,
        send_sem=halo_send.at[0],
        recv_sem=halo_recv.at[0],
        device_id={"gx": east},
        device_id_type=MESH,
    )
    to_west = pltpu.make_async_remote_copy(
        src_ref=pack.at[1],
        dst_ref=east_ref,
        send_sem=halo_send.at[1],
        recv_sem=halo_recv.at[1],
        device_id={"gx": west},
        device_id_type=MESH,
    )
    to_east.start()
    to_west.start()

    for j in range(ATY):

        @pl.when(first_target + j != me)
        def _():
            piece_copy(j).wait_send()

    for b in range(ATY):
        pltpu.make_async_copy(table_ref.at[b], table_ref.at[b], piece_recv.at[b]).wait()
    to_east.wait()
    to_west.wait()


def wave_kernel(
    bands,
    spec_hbm,
    sea_ref,
    courant_ref,
    phase_ref,
    rate_ref,
    decay_ref,
    tile_ref,
    cell_ref,
    weight_ref,
    table_ref,
    west_ref,
    east_ref,
    out_hbm,
    stress_ref,
    spec,
    out,
    stage,
    along_ref,
    lane_hot,
    row_hot,
    in_sem,
    out_sem,
):
    freqs, dirs = spec.shape[0], spec.shape[1]
    chunks = freqs // FCHUNK
    cosine, sine, forward, backward = directions(dirs)
    slots = 2 * len(forward)

    def load(g):
        span = pl.ds(g * FCHUNK, FCHUNK)
        return pltpu.make_async_copy(spec_hbm.at[span], spec.at[span], in_sem.at[g])

    def store(g):
        span = pl.ds(g * FCHUNK, FCHUNK)
        return pltpu.make_async_copy(out.at[span], out_hbm.at[span], out_sem.at[g])

    for g in range(chunks):
        load(g).start()

    lane, row = lane_row((8, 128))
    sea = sea_ref[...].astype(jnp.float32)

    tile = [tile_ref[l] for l in range(4)]
    cell = [cell_ref[l] for l in range(4)]
    weight = [weight_ref[l] for l in range(4)]
    low = [c & 127 for c in cell]
    high = []
    for l in range(4):
        band = jnp.zeros((8, 128), jnp.int32)
        for b in range(1, ATY):
            band = band + (tile[l] >= b * bands).astype(jnp.int32)
        high.append(band * 8 + (cell[l] >> 7))

    forcing = [[jnp.zeros((8, 128), jnp.float32) for _ in range(4)] for _ in range(4)]
    for h in range(32):
        b, r, c = h // 8, h % 8 // 2, h % 2
        hit = [high[l] == h for l in range(4)]
        for k in range(4):
            line = jnp.broadcast_to(table_ref[b, k, pl.ds(r, 1), pl.ds(c * 128, 128)], (8, 128))
            for l in range(4):
                found = jnp.take_along_axis(line, low[l], axis=1)
                forcing[k][l] = jnp.where(hit[l], found, forcing[k][l])
    east_wind, north_wind, air, stability = [
        (weight[0] * v[0] + weight[1] * v[1]) + (weight[2] * v[2] + weight[3] * v[3])
        for v in forcing
    ]
    for d in range(dirs):
        along_ref[d] = float(cosine[d]) * east_wind + float(sine[d]) * north_wind

    lows = lax.broadcasted_iota(jnp.int32, (128, 128), 0)
    for l in range(4):
        for y in range(8):
            at = pl.ds((l * 8 + y) * 128, 128)
            same = lows == jnp.broadcast_to(low[l][y : y + 1], (128, 128))
            lane_hot[:, at] = jnp.where(same, 1.0, 0.0).astype(jnp.bfloat16)

    first, last = lane == 0, lane == 127
    bottom, top = row == 0, row == 7

    sides = ((forward, west_ref), (backward, east_ref))
    for c in range(chunks):
        for side in range(2):
            for fi in range(FCHUNK):
                halo = sides[side][1][fi]
                if c:
                    halo = pltpu.roll(halo, 128 - c * slots, 1)
                stage[side, c * FCHUNK + fi] = halo
    for k in range(len(forward)):
        for side in range(2):
            members = sides[side][0]
            if k >= len(members):
                continue
            for c in range(chunks):
                rolled = [
                    pltpu.roll(stage[side, c * FCHUNK + fi], 127 - 2 * k, 1)
                    for fi in range(FCHUNK)
                ]
                for fi in range(FCHUNK):
                    out[c * FCHUNK + fi, members[k]] = rolled[fi]

    def propagate(c, energy):
        load(c).wait()
        sums = [energy] + [jnp.zeros((8, 128), jnp.float32) for _ in range(3)]
        speeds = [courant_ref[c * FCHUNK + fi] for fi in range(FCHUNK)]
        for side, members in enumerate((forward, backward)):
            shift = 1 if side == 0 else 127
            for d in members:
                done = []
                for fi in range(FCHUNK):
                    step_x = speeds[fi] * float(abs(cosine[d]))
                    step_y = speeds[fi] * float(abs(sine[d]))
                    keep = 1.0 - step_x - step_y
                    halo = out[c * FCHUNK + fi, d]
                    field = spec[c * FCHUNK + fi, d] * sea
                    for substep in range(2):
                        if substep == 0:
                            upwind = jnp.where(last if side == 0 else first, halo, field)
                            upwind = pltpu.roll(upwind, shift, 1)
                        else:
                            upwind = pltpu.roll(field, shift, 1)
                            upwind = jnp.where(first if side == 0 else last, halo, upwind)
                        result = keep * field + step_x * upwind
                        if sine[d] != 0:
                            up = sine[d] > 0
                            beside = pltpu.roll(field, 1 if up else 7, 0)
                            beside = jnp.where(bottom if up else top, 0.0, beside)
                            result = result + step_y * beside
                        field = sea * result
                    done.append(field)
                for fi, field in enumerate(done):
                    out[c * FCHUNK + fi, d] = field
                    sums[fi % 4] = sums[fi % 4] + field
        return (sums[0] + sums[1]) + (sums[2] + sums[3])

    energy = lax.fori_loop(0, chunks, propagate, jnp.zeros((8, 128), jnp.float32))

    base = air * jnp.exp(0.3 * stability)

    def sources(g, stress):
        sums = [stress] + [jnp.zeros((8, 128), jnp.float32) for _ in range(3)]
        for fi in range(FCHUNK):
            f = g * FCHUNK + fi
            offset = rate_ref[f] * base
            slope = offset / phase_ref[f]
            scale = 1.0 / (1.0 + decay_ref[f] * energy)
            for d in range(dirs):
                growth = jnp.maximum(along_ref[d] * slope - offset, 0.0)
                scaled = out[f, d] * scale
                updated = scaled + scaled * growth
                out[f, d] = updated
                sums[d % 4] = sums[d % 4] + growth * updated
        store(g).start()
        return (sums[0] + sums[1]) + (sums[2] + sums[3])

    stress = lax.fori_loop(0, chunks, sources, jnp.zeros((8, 128), jnp.float32))

    surface = sea * (0.01 * (east_wind * east_wind + north_wind * north_wind + stress))
    highs = lax.broadcasted_iota(jnp.int32, (32, 128), 0)
    for l in range(4):
        rest = weight[l] * surface
        parts = []
        for _ in range(3):
            part = rest.astype(jnp.bfloat16).astype(jnp.float32)
            parts.append(part)
            rest = rest - part
        for y in range(8):
            at = pl.ds((l * 8 + y) * 128, 128)
            same = highs == jnp.broadcast_to(high[l][y : y + 1], (32, 128))
            for p, part in enumerate(parts):
                line = jnp.broadcast_to(part[y : y + 1], (32, 128))
                row_hot[pl.ds(p * 32, 32), at] = jnp.where(same, line, 0.0).astype(jnp.bfloat16)
    spread = lax.dot_general(
        row_hot[...],
        lane_hot[...],
        (((1,), (1,)), ((), ())),
        preferred_element_type=jnp.float32,
    )
    stress_ref[...] = spread[0:32] + (spread[32:64] + spread[64:96])

    for g in range(chunks):
        store(g).wait()


def return_kernel(ranks, stress_ref, out_ref, landed, send_sem, recv_sem):
    me = lax.axis_index("gx")
    bands = ranks // ATY
    group = me // ATY
    slot = lax.rem(me, ATY)
    first_source = lax.rem(me, bands) * ATY
    own = lax.rem(me, bands) == group
    barrier = pltpu.get_barrier_semaphore()
    for j in range(ATY):

        @pl.when(first_source + j != me)
        def _():
            pl.semaphore_signal(
                barrier, inc=1, device_id={"gx": first_source + j}, device_id_type=MESH
            )

    pl.semaphore_wait(barrier, ATY - own.astype(jnp.int32))

    def piece(b):
        return stress_ref.at[pl.ds(b * 8, 8)]

    def piece_copy(b):
        return pltpu.make_async_remote_copy(
            src_ref=piece(b),
            dst_ref=landed.at[slot],
            send_sem=send_sem.at[b],
            recv_sem=recv_sem.at[slot],
            device_id={"gx": b * bands + group},
            device_id_type=MESH,
        )

    for b in range(ATY):

        @pl.when(b * bands + group != me)
        def _():
            piece_copy(b).start()

        @pl.when(b * bands + group == me)
        def _():
            pltpu.make_async_copy(piece(b), landed.at[slot], recv_sem.at[slot]).start()

    for j in range(ATY):
        pltpu.make_async_copy(landed.at[j], landed.at[j], recv_sem.at[j]).wait()
        for r in range(4):
            for c in range(2):
                out_ref[0, pl.ds(r, 1), pl.ds(j * 256 + c * 128, 128)] = landed[
                    j, pl.ds(2 * r + c, 1), :
                ]
    for b in range(ATY):

        @pl.when(b * bands + group != me)
        def _():
            piece_copy(b).wait_send()


def on_device(
    ranks,
    spectrum,
    sea_mask,
    courant,
    phase_speed,
    growth_rate,
    dissipation,
    atmos_fields,
    intersection_tile,
    intersection_cell,
    intersection_weight,
):
    freqs, dirs, lat, width = spectrum.shape
    chunks = freqs // FCHUNK
    bands = ranks // ATY
    f32 = jnp.float32
    _, _, forward, _ = directions(dirs)
    consts = jnp.asarray(pack_constants(dirs, 2 * len(forward), chunks))
    anywhere = pl.BlockSpec(memory_space=pltpu.HBM)
    vmem = pl.BlockSpec(memory_space=pltpu.VMEM)
    smem = pl.BlockSpec(memory_space=pltpu.SMEM)
    dma = pltpu.SemaphoreType.DMA
    span = atmos_fields.shape[3] // ATY
    halo = jax.ShapeDtypeStruct((FCHUNK, lat, width), f32)
    table, west, east = pl.pallas_call(
        functools.partial(exchange_kernel, ranks),
        out_shape=(
            jax.ShapeDtypeStruct((ATY,) + atmos_fields.shape[1:3] + (span,), f32),
            halo,
            halo,
        ),
        in_specs=[anywhere, vmem, smem, vmem, anywhere],
        out_specs=(anywhere, anywhere, anywhere),
        scratch_shapes=[
            pltpu.VMEM(spectrum.shape, f32),
            pltpu.VMEM((2, freqs, lat, width), f32),
            pltpu.VMEM((2, FCHUNK, lat, width), f32),
            dma((chunks,)),
            dma((ATY,)),
            dma((ATY,)),
            dma((2,)),
            dma((2,)),
        ],
        compiler_params=pltpu.CompilerParams(
            collective_id=0, has_side_effects=True, vmem_limit_bytes=62 * 2**20
        ),
        name="exchange",
    )(spectrum, sea_mask, courant, consts, atmos_fields)

    updated, stress = pl.pallas_call(
        functools.partial(wave_kernel, bands),
        out_shape=(
            jax.ShapeDtypeStruct(spectrum.shape, f32),
            jax.ShapeDtypeStruct((32, 128), f32),
        ),
        in_specs=[anywhere, vmem, smem, smem, smem, smem] + [vmem] * 6,
        out_specs=(anywhere, vmem),
        scratch_shapes=[
            pltpu.VMEM(spectrum.shape, f32),
            pltpu.VMEM(spectrum.shape, f32),
            pltpu.VMEM((2, freqs, lat, width), f32),
            pltpu.VMEM((dirs, lat, width), f32),
            pltpu.VMEM((128, 32 * 128), jnp.bfloat16),
            pltpu.VMEM((96, 32 * 128), jnp.bfloat16),
            dma((chunks,)),
            dma((chunks,)),
        ],
        compiler_params=pltpu.CompilerParams(vmem_limit_bytes=62 * 2**20),
        name="wave",
    )(
        spectrum,
        sea_mask,
        courant,
        phase_speed,
        growth_rate,
        dissipation,
        intersection_tile,
        intersection_cell,
        intersection_weight,
        table,
        west,
        east,
    )

    roughness = pl.pallas_call(
        functools.partial(return_kernel, ranks),
        out_shape=jax.ShapeDtypeStruct((1,) + atmos_fields.shape[2:], f32),
        in_specs=[anywhere],
        out_specs=vmem,
        scratch_shapes=[
            pltpu.VMEM((ATY, 8, 128), f32),
            dma((ATY,)),
            dma((ATY,)),
        ],
        compiler_params=pltpu.CompilerParams(collective_id=1, has_side_effects=True, vmem_limit_bytes=62 * 2**20),
        name="give_back",
    )(stress)
    return (updated, roughness)


def solution(mesh):
    in_specs = (
        P(None, None, "groups", "gx"),
        P("groups", "gx"),
        P(),
        P(),
        P(),
        P(),
        P("gx", None, "groups", None),
        P(None, "groups", "gx"),
        P(None, "groups", "gx"),
        P(None, "groups", "gx"),
    )
    out_specs = (P(None, None, "groups", "gx"), P("gx", "groups", None))
    return jax.shard_map(
        functools.partial(on_device, mesh.shape["gx"]),
        mesh=mesh,
        in_specs=in_specs,
        out_specs=out_specs,
        check_vma=False,
    )
```
